512 devices in a mesh: diag: 32 (over x_lo, z), tile: 16 (over y, x_hi, core).
Axes of the slice: x: 4 (x_hi: 2, x_lo: 2; x = x_hi * 2 + x_lo), y: 4, z: 16, core: 2. Of those that a mesh axis runs over, the one named last changes fastest.
Arguments:
- tiles: bfloat16 [32, 16, 1280, 1280], P('diag', 'tile'), may hold values from -0.03125 to 0.03125
- live_groups: int32 [32, 16], P('diag', 'tile'), may hold values from 1 to 10, as said below
- vectors: bfloat16 [40960, 256], P('diag'), may hold values from -6 to 6
- previous: float32 [40960, 256], P('diag', 'tile'), may hold values from -6 to 6
- energies: float32 [40960], P('diag'), may hold values from 0.5 to 8
- beta_prev: float32 [256], P('tile'), may hold values from 0.3 to 1.5
Outputs:
- next_vector: float32 [40960, 256], P('diag', 'tile')
- alpha: float32 [256], P('tile')
- beta: float32 [256], P('tile')
The draws below stay inside these ranges and needn't reach their ends.
Inputs may be any that keep to these rules, and one draw needn't show every extreme that they name: `live_groups`: every stored tile has at least one live group; in every draw some tile is fully live.
All inputs are finite; a program needn't handle non-finite values.
Results may differ from the reference program's by a relative error of at most 0.0015.
Values may be sent and summed in bfloat16 or wider, within the bound.
A program may use at most 64 MiB of HBM per device.

```python
import math
import jax
import jax.numpy as jnp
from jax import lax

B = 1280
K = 256
GROUP = 128
N = 40960
N_DIAG = 32
N_TILE = 16


def draw_live_groups(key, part):
    key = jax.random.fold_in(key, 7)
    first, second, third = jax.random.split(key, 3)
    counts = jax.random.randint(first, (N_DIAG, N_TILE), 1, B // GROUP + 1).astype(jnp.int32)
    row_pick = jax.random.randint(second, (), 0, N_DIAG)
    col_pick = jax.random.randint(third, (), 0, N_TILE)
    return counts.at[row_pick, col_pick].set(B // GROUP)


def levels(own_key, extent, cuts, least, largest):
    factor_of, own = 1.0, jax.random.fold_in(own_key, 6)
    for dim, shards_of in cuts:
        draws = jnp.exp(jax.random.uniform(jax.random.fold_in(own, dim), (shards_of,), jnp.float32, least / len(cuts), largest / len(cuts)))
        factor_of = factor_of * jnp.repeat(draws, extent[dim] // shards_of).reshape([-1 if axis == dim else 1 for axis in range(len(extent))])
    return factor_of


def scatter_about(own_key, dims, deviation, bound, cuts=(), kind=jnp.bfloat16):
    result = deviation * jax.random.normal(own_key, dims, jnp.float32)
    if cuts:
        result = result * levels(own_key, dims, cuts, -0.22, 0.18)
    return jnp.clip(result, -bound, bound).astype(kind)


def setup_inputs(seed: int = 0) -> dict:
    arg_keys = jax.random.split(jax.random.key(seed), 7)
    tiles = scatter_about(arg_keys[0], (N_DIAG, N_TILE, B, B), (2 * B * N_TILE) ** -0.5, 0.03125, ((0, 32), (1, 16)))
    live_groups = draw_live_groups(jax.random.fold_in(arg_keys[6], 71), 0)
    vectors = scatter_about(arg_keys[2], (N, K), 1.0, 6.0, ((0, 32),))
    previous = scatter_about(arg_keys[3], (N, K), 1.0, 6.0, ((0, 32), (1, 16)), jnp.float32)
    energies = jnp.clip(jnp.exp(math.log(8.0) - 2.7725887 * jax.random.uniform(arg_keys[4], (N,), jnp.float32) ** levels(arg_keys[4], (N,), ((0, 32),), -0.2, 0.2)), 0.5, 8.0)
    beta_prev = jnp.clip(jnp.exp(math.log(1.5) - 1.60943787 * jax.random.uniform(arg_keys[5], (K,), jnp.float32) ** levels(arg_keys[5], (K,), ((0, 16),), -0.2, 0.2)), 0.3, 1.5)
    return {"tiles": tiles, "live_groups": live_groups, "vectors": vectors, "previous": previous, "energies": energies, "beta_prev": beta_prev}


def reference(tiles, live_groups, vectors, previous, energies, beta_prev):
    vf = vectors.astype(jnp.float32).reshape(N_DIAG, B, K)
    rows = jnp.arange(B, dtype=jnp.int32)
    hv = jnp.zeros((N_DIAG, B, K), jnp.float32)
    for q in range(N_TILE):
        live = (rows[None, :] < GROUP * live_groups[:, q][:, None]).astype(jnp.float32)
        tile_f = tiles[:, q].astype(jnp.float32)
        source = jnp.roll(vf, q, axis=0)
        direct = jnp.einsum('pij,pjk->pik', tile_f, source) * live[:, :, None]
        masked = vf * live[:, :, None]
        turned = jnp.einsum('pji,pjk->pik', tile_f, masked)
        hv = hv + direct + jnp.roll(turned, -q, axis=0)
    flat = vf.reshape(N_DIAG * B, K)
    hv = hv.reshape(N_DIAG * B, K) + energies[:, None] * flat
    alpha = lax.optimization_barrier(jnp.sum(flat * hv, axis=0)) / lax.optimization_barrier(jnp.sum(flat * flat, axis=0))
    resid = hv - alpha[None, :] * flat - beta_prev[None, :] * previous
    beta = jnp.sqrt(lax.optimization_barrier(jnp.mean(resid * resid, axis=0)) + 1e-06)
    return (resid / beta[None, :], alpha, beta)
```

```python
import functools

import jax
import jax.numpy as jnp
from jax import lax
from jax.experimental import pallas as pl
from jax.experimental.pallas import tpu as pltpu
from jax.sharding import PartitionSpec as P

GROUP = 128
MESH = pl.DeviceIdType.MESH
F32 = jnp.float32
BF16 = jnp.bfloat16


def tree_of(nt):
    if nt == 16:
        nodes = [(0, None), (3, 0), (-3, 0), (6, 1), (-6, 2)]
    elif nt == 4:
        nodes = [(0, None), (1, 0), (2, 1)]
    else:
        nodes = [(0, None)]
    offsets = range(-(nt // 2) + 1, nt // 2 + 1)
    sides = [[] for _ in nodes]
    for off in offsets:
        best = min(range(len(nodes)), key=lambda n: (abs(nodes[n][0] - off), n))
        sides[best].append(off)
    return nodes, sides


def kernel(
    nt, nodes, sides, rows_total,
    live_ref, vec_ref, prev_ref, energy_ref, bprev_ref, tiles_ref,
    out_ref, stat_ref,
    tile, vt, vsrc, turned, direct, tside, drecv, vch, tch, tout, row_out, rows_in,
    tile_sem, vd_send, vd_recv, vc_send, vc_recv, td_send, td_recv, tc_send, tc_recv,
    dd_send, dd_recv, st_send, st_recv,
):
    nd = 2 * nt
    size = vec_ref.shape[0]
    share = vt.shape[1]
    me_p = lax.axis_index("diag")
    me_q = lax.axis_index("tile")
    z = lax.rem(me_p, nt)
    a = lax.div(me_p, nt)
    n_nodes = len(nodes)

    load_tile = pltpu.make_async_copy(tiles_ref.at[0, 0], tile, tile_sem)
    load_tile.start()

    def plane(shift):
        return nt * a + lax.rem(z + (shift + 2 * nt), nt)

    def dest(n, off):
        home = plane(-nodes[n][0])
        q = off % nt
        return lax.rem(home + q, nd), q

    my_seg = lax.rem(me_p - me_q + nd, nd)
    my_node = jnp.int32(0)
    for n, offs in enumerate(sides):
        for off in offs:
            my_node = my_node + jnp.where(me_q == off % nt, nodes[n][0], 0)
    node_p = nt * lax.div(my_seg, nt) + lax.rem(my_seg + my_node + 2 * nt, nt)

    barrier = pltpu.get_barrier_semaphore()

    def greet(p, q):
        pl.semaphore_signal(barrier, inc=1, device_id=(p, q), device_id_type=MESH)

    expected = jnp.int32(2 * (n_nodes - 1) + (nt - 1) + (nd - 1) + 2 * nt)
    for n, (off, parent) in enumerate(nodes):
        if parent is not None:
            step = off - nodes[parent][0]
            greet(plane(step), me_q)
            greet(plane(-step), me_q)
    for n, offs in enumerate(sides):
        for off in offs:
            p, q = dest(n, off)
            if off == nodes[n][0]:
                itself = jnp.logical_and(p == me_p, q == me_q)
                expected = expected - jnp.where(itself, 2, 0)

                @pl.when(jnp.logical_not(itself))
                def _():
                    greet(p, q)
            else:
                greet(p, q)

    @pl.loop(0, nt)
    def _(j):
        @pl.when(jnp.logical_not(jnp.logical_and(node_p == me_p, j == me_q)))
        def _():
            greet(node_p, j)

    @pl.loop(1, nt)
    def _(j):
        greet(me_p, lax.rem(me_q + j, nt))

    @pl.loop(1, nd)
    def _(d):
        greet(lax.rem(me_p + d, nd), me_q)

    vt[...] = vec_ref[...].T.reshape(nt, share, size)
    pl.semaphore_wait(barrier, expected)

    def remote(src, dst, send, recv, p, q):
        return pltpu.make_async_remote_copy(
            src_ref=src, dst_ref=dst, send_sem=send, recv_sem=recv,
            device_id=(p, q), device_id_type=MESH,
        )

    def v_piece(n):
        return vt.at[me_q] if n == 0 else vch.at[n - 1]

    def v_forward(n):
        for m, (off, parent) in enumerate(nodes):
            if parent == n:
                remote(
                    v_piece(n), vch.at[m - 1], vc_send.at[m - 1], vc_recv.at[m - 1],
                    plane(off - nodes[n][0]), me_q,
                ).start()

    def v_deliver_copy(n, off):
        p, q = dest(n, off)
        return remote(
            v_piece(n), vsrc.at[me_q], vd_send.at[q], vd_recv.at[me_q], p, q
        ), jnp.logical_and(p == me_p, q == me_q)

    def v_deliver(n):
        for off in sides[n]:
            copy, itself = v_deliver_copy(n, off)
            if off == nodes[n][0]:
                @pl.when(itself)
                def _():
                    pltpu.make_async_copy(v_piece(n), vsrc.at[me_q], vd_recv.at[me_q]).start()

                @pl.when(jnp.logical_not(itself))
                def _():
                    copy.start()
            else:
                copy.start()

    def arrived(ref, sem):
        pltpu.make_async_copy(ref, ref, sem).wait()

    v_forward(0)
    v_deliver(0)

    live = live_ref[0, 0] * GROUP
    load_tile.wait()
    flat = vt[...].reshape(nt * share, size)
    lanes = lax.broadcasted_iota(jnp.int32, flat.shape, 1)
    masked = jnp.where(lanes < live, flat, jnp.zeros_like(flat))
    wide = 256 if size % 256 == 0 else 128

    @pl.loop(0, size // wide)
    def _(b):
        cols = pl.ds(pl.multiple_of(b * wide, wide), wide)
        prod = jnp.dot(masked, tile[:, cols], preferred_element_type=F32)
        turned[:, :, cols] = prod.astype(BF16).reshape(nt, share, wide)

    for n in range(1, n_nodes):
        arrived(vch.at[n - 1], vc_recv.at[n - 1])
        v_forward(n)
        v_deliver(n)

    def t_copy(j):
        return remote(
            turned.at[j], tside.at[me_q], td_send.at[j], td_recv.at[me_q], node_p, j
        ), jnp.logical_and(node_p == me_p, j == me_q)

    @pl.loop(0, nt)
    def _(i):
        j = lax.rem(i + me_q, nt)
        copy, itself = t_copy(j)

        @pl.when(itself)
        def _():
            pltpu.make_async_copy(turned.at[j], tside.at[me_q], td_recv.at[me_q]).start()

        @pl.when(jnp.logical_not(itself))
        def _():
            copy.start()

    @pl.loop(0, nt)
    def _(j):
        arrived(vsrc.at[j], vd_recv.at[j])

    source = vsrc[...].reshape(nt * share, size)

    @pl.loop(0, size // wide)
    def _(b):
        first = pl.multiple_of(b * wide, wide)
        part = pl.ds(first, wide)
        prod = lax.dot_general(
            source, tile[part, :], (((1,), (1,)), ((), ())), preferred_element_type=F32
        )
        spot = lax.broadcasted_iota(jnp.int32, prod.shape, 1) + first
        prod = jnp.where(spot < live, prod, 0.0)
        direct[:, :, part] = prod.astype(BF16).reshape(nt, share, wide)

    def d_copy(j):
        return remote(
            direct.at[j], drecv.at[me_q], dd_send.at[j], dd_recv.at[me_q], me_p, j
        )

    @pl.loop(1, nt)
    def _(i):
        d_copy(lax.rem(i + me_q, nt)).start()

    def t_up(n):
        off, parent = nodes[n]
        return remote(
            tout.at[n - 1], tch.at[n - 1], tc_send.at[n - 1], tc_recv.at[n - 1],
            plane(nodes[parent][0] - off), me_q,
        )

    total = None
    for n in reversed(range(n_nodes)):
        total = jnp.zeros((share, size), F32)
        for off in sides[n]:
            arrived(tside.at[off % nt], td_recv.at[off % nt])
            total = total + tside[off % nt].astype(F32)
        for m, (_, parent) in enumerate(nodes):
            if parent == n:
                arrived(tch.at[m - 1], tc_recv.at[m - 1])
                total = total + tch[m - 1].astype(F32)
        if n > 0:
            tout[n - 1] = total.astype(BF16)
            t_up(n).start()

    total = total + direct[me_q].astype(F32)

    def add_direct(i, acc):
        j = lax.rem(i + me_q, nt)
        arrived(drecv.at[j], dd_recv.at[j])
        return acc + drecv[j].astype(F32)

    total = lax.fori_loop(1, nt, add_direct, total)

    own = vt[me_q].astype(F32)
    hv = total + energy_ref[...] * own
    line = lax.broadcasted_iota(jnp.int32, (share, 128), 0)
    lane = lax.broadcasted_iota(jnp.int32, (share, 128), 1)

    def as_row(column, slot):
        return jnp.sum(jnp.where(lane == line + slot * share, column, 0.0), axis=0, keepdims=True)

    def as_column(row):
        return jnp.sum(jnp.where(lane == line, row, 0.0), axis=1, keepdims=True)

    w = hv - as_column(bprev_ref[...]) * prev_ref[...]
    numer = jnp.sum(own * hv, axis=1, keepdims=True)
    norm = jnp.sum(own * own, axis=1, keepdims=True)
    slope = jnp.sum(own * w, axis=1, keepdims=True) / jnp.where(norm > 0.0, norm, 1.0)
    rest = w - slope * own
    rest = jnp.sum(rest * rest, axis=1, keepdims=True)
    row_out[0] = as_row(numer, 0) + as_row(norm, 1) + as_row(slope, 2) + as_row(rest, 3)
    rows_in[me_p] = row_out[0]

    def s_copy(d):
        p = lax.rem(me_p + d, nd)
        return remote(
            row_out.at[0], rows_in.at[me_p], st_send.at[d], st_recv.at[me_p], p, me_q
        )

    @pl.loop(1, nd)
    def _(d):
        s_copy(d).start()

    @pl.loop(1, nd)
    def _(d):
        p = lax.rem(me_p + d, nd)
        arrived(rows_in.at[p], st_recv.at[p])

    rows = rows_in[...].reshape(nd, 128)
    norms = pltpu.roll(rows, 128 - share, 1)
    slopes = pltpu.roll(rows, 128 - 2 * share, 1)
    rests = pltpu.roll(rows, 128 - 3 * share, 1)
    alpha = jnp.sum(rows, axis=0, keepdims=True) / jnp.sum(norms, axis=0, keepdims=True)
    gap = slopes - alpha
    squared = jnp.sum(rests + gap * norms * gap, axis=0, keepdims=True)
    beta = jnp.sqrt(squared / rows_total + 1e-06)
    stat_ref[0:1, :] = alpha
    stat_ref[1:2, :] = beta
    out_ref[...] = (w - as_column(alpha) * own) / as_column(beta)

    for n in range(n_nodes):
        for off in sides[n]:
            copy, itself = v_deliver_copy(n, off)
            if off == nodes[n][0]:
                @pl.when(jnp.logical_not(itself))
                def _():
                    copy.wait_send()
            else:
                copy.wait_send()
        if n > 0:
            t_up(n).wait_send()
            off, parent = nodes[n]
            remote(
                v_piece(parent), vch.at[n - 1], vc_send.at[n - 1], vc_recv.at[n - 1],
                plane(off - nodes[parent][0]), me_q,
            ).wait_send()

    @pl.loop(0, nt)
    def _(j):
        copy, itself = t_copy(j)

        @pl.when(jnp.logical_not(itself))
        def _():
            copy.wait_send()

    @pl.loop(1, nt)
    def _(i):
        d_copy(lax.rem(i + me_q, nt)).wait_send()

    @pl.loop(1, nd)
    def _(d):
        s_copy(d).wait_send()


def body(tiles, live_groups, vectors, previous, energies, beta_prev):
    nt = lax.axis_size("tile")
    nd = lax.axis_size("diag")
    size, columns = vectors.shape
    share = columns // nt
    nodes, sides = tree_of(nt)
    extra = max(len(nodes) - 1, 1)
    vmem = pl.BlockSpec(memory_space=pltpu.VMEM)
    dma = pltpu.SemaphoreType.DMA
    bprev = jnp.pad(beta_prev, (0, 128 - share))[None, :]
    out, stat = pl.pallas_call(
        functools.partial(kernel, nt, nodes, sides, float(size * nd)),
        out_shape=(
            jax.ShapeDtypeStruct((share, size), F32),
            jax.ShapeDtypeStruct((2, 128), F32),
        ),
        in_specs=[
            pl.BlockSpec(memory_space=pltpu.SMEM), vmem, vmem, vmem, vmem,
            pl.BlockSpec(memory_space=pl.ANY),
        ],
        out_specs=(vmem, vmem),
        scratch_shapes=[
            pltpu.VMEM((size, size), BF16),
            pltpu.VMEM((nt, share, size), BF16),
            pltpu.VMEM((nt, share, size), BF16),
            pltpu.VMEM((nt, share, size), BF16),
            pltpu.VMEM((nt, share, size), BF16),
            pltpu.VMEM((nt, share, size), BF16),
            pltpu.VMEM((nt, share, size), BF16),
            pltpu.VMEM((extra, share, size), BF16),
            pltpu.VMEM((extra, share, size), BF16),
            pltpu.VMEM((extra, share, size), BF16),
            pltpu.VMEM((1, 1, 128), F32),
            pltpu.VMEM((nd, 1, 128), F32),
            dma, dma((nt,)), dma((nt,)), dma((extra,)), dma((extra,)),
            dma((nt,)), dma((nt,)), dma((extra,)), dma((extra,)),
            dma((nt,)), dma((nt,)), dma((nd,)), dma((nd,)),
        ],
        compiler_params=pltpu.CompilerParams(
            collective_id=0, has_side_effects=True, vmem_limit_bytes=40 * 1024 * 1024
        ),
    )(live_groups, vectors, previous.T, energies[None, :], bprev, tiles)
    return out.T, stat[0, :share], stat[1, :share]


def solution(mesh):
    return jax.shard_map(
        body,
        mesh=mesh,
        in_specs=(
            P("diag", "tile", None, None),
            P("diag", "tile"),
            P("diag", None),
            P("diag", "tile"),
            P("diag"),
            P("tile"),
        ),
        out_specs=(P("diag", "tile"), P("tile"), P("tile")),
        check_vma=False,
    )
```

```python
import functools

import jax
import jax.numpy as jnp
from jax import lax
from jax.experimental import pallas as pl
from jax.experimental.pallas import tpu as pltpu
from jax.sharding import PartitionSpec as P

GROUP = 128
MESH = pl.DeviceIdType.MESH
F32 = jnp.float32
BF16 = jnp.bfloat16
ORDER = ((1, 0), (3, 0), (0, 1), (2, 0), (1, 1), (3, 1), (2, 1))
VMEM_MIB = 58
PLAN = (('v', 0), ('product', 0), ('t', 6), ('v', 1), ('v', 2), ('t', 4), ('turn', 0), ('v', 3), ('v', 4), ('t', 6), ('node', 5), ('node', 3), ('node', 4), ('d', 0), ('d', 1), ('share', 0), ('node', 1), ('node', 2))
SMALL = (("v", 0), ("product", 0), ("t", 2), ("v", 1), ("turn", 0), ("v", 2), ("t", 2), ("node", 1), ("d", 0), ("d", 1), ("node", 2), ("share", 0))


def offsets_of(nt):
    return range(-(nt // 2) + 1, nt // 2 + 1)


def tree_of(nt, nodes):
    sides = [[] for _ in nodes]
    for off in offsets_of(nt):
        best = min(range(len(nodes)), key=lambda n: (abs(nodes[n][0] - off), n))
        sides[best].append(off)
    return nodes, sides


def trees_of(nt):
    if nt == 16:
        chain = [(0, None), (3, 0), (-3, 0), (6, 1), (-6, 2)]
        return tree_of(nt, chain), tree_of(nt, chain + [(8, 0)])
    if nt == 4:
        return tree_of(nt, [(0, None), (1, 0), (2, 1)]), tree_of(nt, [(0, None), (1, 0), (-1, 0)])
    return tree_of(nt, [(0, None)]), tree_of(nt, [(0, None)])


def kernel(
    nt, v_tree, t_tree, rows_total,
    live_ref, energy_ref, bprev_ref, vec_ref, prev_ref, tiles_ref,
    out_ref, alpha_ref, beta_ref,
    vec, prev, tile, flipped, vt, vsrc, turned, tside, dpart, dxch, dsend, drecv, vch, tch, tout,
    row_out, rows_in,
    vec_sem, prev_sem, tile_sem,
    vd_send, vd_recv, vc_send, vc_recv, td_send, td_recv, tc_send, tc_recv,
    dx_send, dx_recv, dd_send, dd_recv, s_send, s_recv,
):
    nd = 2 * nt
    ny = nt // 4
    size = vec_ref.shape[0]
    share = vt.shape[1]
    me_p = lax.axis_index("diag")
    me_q = lax.axis_index("tile")
    z = lax.rem(me_p, nt)
    a = lax.div(me_p, nt)
    core = lax.rem(me_q, 2)
    chip = lax.div(me_q, 2)
    across = lax.rem(chip, 2)
    y = lax.div(chip, 2)
    v_nodes, v_sides = v_tree
    t_nodes, t_sides = t_tree

    load_vec = pltpu.make_async_copy(vec_ref, vec, vec_sem)
    load_vec.start()
    load_tile = pltpu.make_async_copy(tiles_ref.at[0, 0], tile, tile_sem)
    load_tile.start()
    load_prev = pltpu.make_async_copy(prev_ref, prev, prev_sem)
    load_prev.start()

    def plane(shift):
        return nt * a + lax.rem(z + (shift + 2 * nt), nt)

    def dest(nodes, n, off):
        home = plane(-nodes[n][0])
        q = lax.rem(off + nt, nt)
        p = lax.rem(home + q, nd)
        return p, q, jnp.logical_and(p == me_p, q == me_q)

    my_seg = lax.rem(me_p - me_q + nd, nd)

    def node_plane(nodes, sides):
        shift = jnp.int32(0)
        for n, offs in enumerate(sides):
            for off in offs:
                shift = shift + jnp.where(me_q == off % nt, nodes[n][0], 0)
        return nt * lax.div(my_seg, nt) + lax.rem(my_seg + shift + 2 * nt, nt)

    v_from = node_plane(v_nodes, v_sides)
    t_to = node_plane(t_nodes, t_sides)

    def chip_at(dy, db):
        row = lax.rem(y + dy + (ny - 2 * dy) * core + ny, ny)
        return 2 * row + lax.rem(across + db, 2)

    moves = [(dy, db) for dy, db in ORDER if dy < ny]
    spots = [(dy, db, dc) for dc in range(2) for dy, db in moves + [(0, 0)]]

    def tile_at(dy, db, dc):
        return 2 * chip_at(dy, db) + lax.rem(core + dc, 2)

    shifts = sorted(range(1, nt), key=lambda d: -min(d, nt - d)) + [0]
    others = [(da, dz) for dz in shifts for da in (1, 0) if (da, dz) != (0, 0)]

    def segment(da, dz):
        return nt * lax.rem(a + da, 2) + lax.rem(z + dz, nt)

    barrier = pltpu.get_barrier_semaphore()

    def greet(p, q):
        pl.semaphore_signal(barrier, inc=1, device_id=(p, q), device_id_type=MESH)

    expected = jnp.int32(0)

    def greet_unless(p, q, itself):
        @pl.when(jnp.logical_not(itself))
        def _():
            greet(p, q)

        return jnp.where(itself, 0, 1)

    def greet_tree(nodes, sides, home, v):
        count = jnp.int32(0)
        for n, (off, parent) in enumerate(nodes):
            if parent is not None:
                step = off - nodes[parent][0]
                greet(plane(step), me_q)
                greet(plane(-step), me_q)
                count = count + 2
        for n, offs in enumerate(sides):
            for off in offs:
                count = count + greet_unless(*dest(nodes, n, off))
        for j in range(nt):
            count = count + greet_unless(home, j, jnp.logical_and(home == me_p, j == me_q))
        return count

    expected = expected + greet_tree(v_nodes, v_sides, v_from, True)
    expected = expected + greet_tree(t_nodes, t_sides, t_to, False)
    greet(me_p, me_q + 1 - 2 * core)
    for dy, db in moves:
        greet(me_p, 2 * chip_at(dy, db) + core)
    for da, dz in others:
        greet(segment(da, dz), me_q)
    expected = expected + (1 + len(moves) + len(others))

    load_vec.wait()
    vt[...] = vec[...].T.reshape(nt, share, size)
    pl.semaphore_wait(barrier, expected)

    def remote(src, dst, send, recv, p, q):
        return pltpu.make_async_remote_copy(
            src_ref=src, dst_ref=dst, send_sem=send, recv_sem=recv,
            device_id=(p, q), device_id_type=MESH,
        )

    def arrived(ref, sem):
        pltpu.make_async_copy(ref, ref, sem).wait()

    def v_piece(n):
        return vt.at[me_q] if n == 0 else vch.at[n - 1]

    def v_hop(m):
        off, parent = v_nodes[m]
        return remote(
            v_piece(parent), vch.at[m - 1], vc_send.at[m - 1], vc_recv.at[m - 1],
            plane(off - v_nodes[parent][0]), me_q,
        )

    def v_forward(n):
        for m, (_, parent) in enumerate(v_nodes):
            if parent == n:
                v_hop(m).start()

    def v_out(n, off):
        p, q, itself = dest(v_nodes, n, off)
        return remote(v_piece(n), vsrc.at[me_q], vd_send.at[q], vd_recv.at[me_q], p, q), itself

    def v_deliver(n):
        count = len(v_sides[n])
        for i in range(count):
            off = v_sides[n][0] + lax.rem(me_q + i, count)
            copy, itself = v_out(n, off)

            @pl.when(itself)
            def _():
                pltpu.make_async_copy(v_piece(n), vsrc.at[me_q], vd_recv.at[me_q]).start()

            @pl.when(jnp.logical_not(itself))
            def _():
                copy.start()

    live = live_ref[0, 0] * GROUP
    wide = 256 if size % 256 == 0 else 128

    def v_stage(n):
        if n > 0:
            arrived(vch.at[n - 1], vc_recv.at[n - 1])
        v_forward(n)
        v_deliver(n)

    def t_product():
        flat = vt[...].reshape(nt * share, size)
        lanes = lax.broadcasted_iota(jnp.int32, flat.shape, 1)
        masked = jnp.where(lanes < live, flat, jnp.zeros_like(flat))
        load_tile.wait()

        @pl.loop(0, size // wide)
        def _(b):
            cols = pl.ds(pl.multiple_of(b * wide, wide), wide)
            prod = jnp.dot(masked, tile[:, cols], preferred_element_type=F32)
            turned[:, :, cols] = prod.astype(BF16).reshape(nt, share, wide)

    def t_turn():
        @pl.loop(0, size // wide)
        def _(b):
            first = pl.multiple_of(b * wide, wide)
            part = pl.ds(first, wide)
            block = tile[part, :].T
            spot = lax.broadcasted_iota(jnp.int32, block.shape, 1) + first
            flipped[:, part] = jnp.where(spot < live, block, jnp.zeros_like(block))

    def t_out(j):
        return remote(
            turned.at[j], tside.at[me_q], td_send.at[j], td_recv.at[me_q], t_to, j
        ), jnp.logical_and(t_to == me_p, j == me_q)

    def t_send(group):
        for spot in group:
            j = tile_at(*spot)
            copy, itself = t_out(j)

            @pl.when(itself)
            def _():
                pltpu.make_async_copy(turned.at[j], tside.at[me_q], td_recv.at[me_q]).start()

            @pl.when(jnp.logical_not(itself))
            def _():
                copy.start()

    def t_up(n):
        off, parent = t_nodes[n]
        return remote(
            tout.at[n - 1], tch.at[n - 1], tc_send.at[n - 1], tc_recv.at[n - 1],
            plane(t_nodes[parent][0] - off), me_q,
        )

    def t_sum(n):
        total = jnp.zeros((share, size), F32)
        for off in t_sides[n]:
            arrived(tside.at[off % nt], td_recv.at[off % nt])
            total = total + tside[off % nt].astype(F32)
        for m, (_, parent) in enumerate(t_nodes):
            if parent == n:
                arrived(tch.at[m - 1], tc_recv.at[m - 1])
                total = total + tch[m - 1].astype(F32)
        return total

    def t_node(n):
        tout[n - 1] = t_sum(n).astype(BF16)
        t_up(n).start()

    half = nt * share // 2
    m_half = nt // 4

    def d_product(h):
        for j in range(h * nt // 2, (h + 1) * nt // 2):
            arrived(vsrc.at[j], vd_recv.at[j])
        source = vsrc[pl.ds(h * nt // 2, nt // 2)].reshape(half, size)

        @pl.loop(0, size // wide)
        def _(b):
            part = pl.ds(pl.multiple_of(b * wide, wide), wide)
            prod = jnp.dot(source, flipped[:, part], preferred_element_type=F32)
            prod = prod.reshape(m_half, 2, share, wide)
            dpart[0, pl.ds(h * m_half, m_half), :, part] = prod[:, 0]
            dpart[1, pl.ds(h * m_half, m_half), :, part] = prod[:, 1]

        d_swap(h).start()

    def d_swap(h):
        part = pl.ds(h * m_half, m_half)
        return remote(
            dpart.at[1 - core, part], dxch.at[part], dx_send.at[h], dx_recv.at[h],
            me_p, me_q + 1 - 2 * core,
        )

    def d_out(dy, db):
        m = chip_at(dy, db)
        return remote(
            dsend.at[m], drecv.at[chip], dd_send.at[m], dd_recv.at[chip], me_p, 2 * m + core
        ), m

    def d_share():
        for h in range(2):
            arrived(dxch.at[pl.ds(h * m_half, m_half)], dx_recv.at[h])
        for dy, db in moves:
            copy, m = d_out(dy, db)
            dsend[m] = (dpart[core, m] + dxch[m]).astype(BF16)
            copy.start()

    at = 0
    for word, number in PLAN if nt == 16 else SMALL:
        if word == "v":
            v_stage(number)
        elif word == "product":
            t_product()
        elif word == "turn":
            t_turn()
        elif word == "t":
            t_send(spots[at : at + number])
            at += number
        elif word == "node":
            t_node(number)
        elif word == "d":
            d_product(number)
        elif word == "share":
            d_share()

    total = t_sum(0) + dpart[core, chip] + dxch[chip]
    for dy, db in moves:
        m = chip_at(dy, db)
        arrived(drecv.at[m], dd_recv.at[m])
        total = total + drecv[m].astype(F32)

    own = vt[me_q].astype(F32)
    hv = total + energy_ref[...].reshape(1, size) * own
    line = lax.broadcasted_iota(jnp.int32, (share, 128), 0)
    lane = lax.broadcasted_iota(jnp.int32, (share, 128), 1)

    def as_row(column, slot):
        return jnp.sum(jnp.where(lane == line + slot * share, column, 0.0), axis=0, keepdims=True)

    def as_column(row):
        return jnp.sum(jnp.where(lane == line, row, 0.0), axis=1, keepdims=True)

    load_prev.wait()
    square = [lax.broadcasted_iota(jnp.int32, (share, share), d) for d in range(2)]
    before = jnp.where(square[0] == square[1], bprev_ref[...].reshape(1, share), 0.0)
    before = jnp.sum(before, axis=1, keepdims=True)
    w = hv - before * prev[...]
    numer = jnp.sum(own * hv, axis=1, keepdims=True)
    norm = jnp.sum(own * own, axis=1, keepdims=True)
    slope = jnp.sum(own * w, axis=1, keepdims=True) / jnp.where(norm > 0.0, norm, 1.0)
    rest = w - slope * own
    rest = jnp.sum(rest * rest, axis=1, keepdims=True)
    row_out[0] = as_row(numer, 0) + as_row(norm, 1) + as_row(slope, 2) + as_row(rest, 3)
    for da, dz in others:
        remote(row_out.at[0], rows_in.at[me_p], s_send, s_recv, segment(da, dz), me_q).start()
    rows_in[me_p] = row_out[0]
    arrived(rows_in.at[pl.ds(0, nd - 1)], s_recv)

    rows = rows_in[...].reshape(nd, 128)
    norms = pltpu.roll(rows, 128 - share, 1)
    slopes = pltpu.roll(rows, 128 - 2 * share, 1)
    rests = pltpu.roll(rows, 128 - 3 * share, 1)
    alpha = jnp.sum(rows, axis=0, keepdims=True) / jnp.sum(norms, axis=0, keepdims=True)
    gap = slopes - alpha
    squared = jnp.sum(rests + gap * norms * gap, axis=0, keepdims=True)
    beta = jnp.sqrt(squared / rows_total + 1e-06)
    alpha_ref[...] = alpha
    beta_ref[...] = beta
    out_ref[...] = (w - as_column(alpha) * own) / as_column(beta)

    for n in range(len(v_nodes)):
        for off in v_sides[n]:
            copy, itself = v_out(n, off)

            @pl.when(jnp.logical_not(itself))
            def _():
                copy.wait_send()

        if n > 0:
            v_hop(n).wait_send()
    for n in range(1, len(t_nodes)):
        t_up(n).wait_send()
    for j in range(nt):
        copy, itself = t_out(j)

        @pl.when(jnp.logical_not(itself))
        def _():
            copy.wait_send()

    for h in range(2):
        d_swap(h).wait_send()
    for dy, db in moves:
        d_out(dy, db)[0].wait_send()
    arrived(rows_in.at[pl.ds(0, nd - 1)], s_send)


def body(tiles, live_groups, vectors, previous, energies, beta_prev):
    nt = lax.axis_size("tile")
    nd = lax.axis_size("diag")
    size, columns = vectors.shape
    share = columns // nt
    v_tree, t_tree = trees_of(nt)
    v_more, t_more = max(len(v_tree[0]) - 1, 1), max(len(t_tree[0]) - 1, 1)
    vmem = pl.BlockSpec(memory_space=pltpu.VMEM)
    hbm = pl.BlockSpec(memory_space=pl.ANY)
    dma = pltpu.SemaphoreType.DMA
    out, alpha, beta = pl.pallas_call(
        functools.partial(kernel, nt, v_tree, t_tree, float(size * nd)),
        out_shape=(
            jax.ShapeDtypeStruct((share, size), F32),
            jax.ShapeDtypeStruct((1, 128), F32),
            jax.ShapeDtypeStruct((1, 128), F32),
        ),
        in_specs=[pl.BlockSpec(memory_space=pltpu.SMEM), vmem, vmem, hbm, hbm, hbm],
        out_specs=(vmem, vmem, vmem),
        scratch_shapes=[
            pltpu.VMEM((size, columns), BF16),
            pltpu.VMEM((share, size), F32),
            pltpu.VMEM((size, size), BF16),
            pltpu.VMEM((size, size), BF16),
            pltpu.VMEM((nt, share, size), BF16),
            pltpu.VMEM((nt, share, size), BF16),
            pltpu.VMEM((nt, share, size), BF16),
            pltpu.VMEM((nt, share, size), BF16),
            pltpu.VMEM((2, nt // 2, share, size), F32),
            pltpu.VMEM((nt // 2, share, size), F32),
            pltpu.VMEM((nt // 2, share, size), BF16),
            pltpu.VMEM((nt // 2, share, size), BF16),
            pltpu.VMEM((v_more, share, size), BF16),
            pltpu.VMEM((t_more, share, size), BF16),
            pltpu.VMEM((t_more, share, size), BF16),
            pltpu.VMEM((1, 1, 128), F32),
            pltpu.VMEM((nd, 1, 128), F32),
            dma, dma, dma,
            dma((nt,)), dma((nt,)), dma((v_more,)), dma((v_more,)),
            dma((nt,)), dma((nt,)), dma((t_more,)), dma((t_more,)),
            dma((2,)), dma((2,)), dma((nt // 2,)), dma((nt // 2,)),
            dma, dma,
        ],
        compiler_params=pltpu.CompilerParams(
            collective_id=0, has_side_effects=True, vmem_limit_bytes=VMEM_MIB * 1024 * 1024
        ),
    )(live_groups, energies, beta_prev, vectors, previous.T, tiles)
    return out.T, alpha[0, :share], beta[0, :share]


def solution(mesh):
    return jax.shard_map(
        body,
        mesh=mesh,
        in_specs=(
            P("diag", "tile", None, None),
            P("diag", "tile"),
            P("diag", None),
            P("diag", "tile"),
            P("diag"),
            P("tile"),
        ),
        out_specs=(P("diag", "tile"), P("tile"), P("tile")),
        check_vma=False,
    )
```

```python
import functools

import jax
import jax.numpy as jnp
from jax import lax
from jax.experimental import pallas as pl
from jax.experimental.pallas import tpu as pltpu
from jax.sharding import PartitionSpec as P

GROUP = 128
MESH = pl.DeviceIdType.MESH
F32 = jnp.float32
BF16 = jnp.bfloat16
ORDER = ((1, 0), (3, 0), (0, 1), (2, 0), (1, 1), (3, 1), (2, 1))
VMEM_MIB = 58
FAR = 3
V_PARTS = 2
T_PARTS = 2
PLAN = (('product', 0), ('greeted', 0), ('v', 0), ('far', 8), ('mid', 8), ('near', 4), ('turn', 0), ('v', 1), ('v', 2), ('far', 8), ('mid', 8), ('v', 3), ('v', 4), ('near', 12), ('node', 5), ('node', 3), ('node', 4), ('d', 0), ('d', 1), ('share', 0), ('node', 1), ('node', 2))
SMALL = (("greeted", 0), ("v", 0), ("product", 0), ("near", 2), ("v", 1), ("turn", 0), ("v", 2), ("near", 2), ("node", 2), ("node", 1), ("d", 0), ("d", 1), ("share", 0))


def offsets_of(nt):
    return range(-(nt // 2) + 1, nt // 2 + 1)


def tree_of(nt, nodes):
    sides = [[] for _ in nodes]
    for off in offsets_of(nt):
        best = min(range(len(nodes)), key=lambda n: (abs(nodes[n][0] - off), n))
        sides[best].append(off)
    return nodes, sides


def trees_of(nt):
    if nt == 16:
        chain = [(0, None), (3, 0), (-3, 0), (6, 1), (-6, 2)]
        return tree_of(nt, chain), tree_of(nt, chain + [(8, FAR)])
    if nt == 4:
        return tree_of(nt, [(0, None), (1, 0), (2, 1)]), tree_of(nt, [(0, None), (1, 0), (2, 1)])
    return tree_of(nt, [(0, None)]), tree_of(nt, [(0, None)])


def kernel(
    nt, v_tree, t_tree, rows_total,
    live_in, energy_in, bprev_in, vec_ref, prev_ref, tiles_ref,
    out_ref, alpha_ref, beta_ref,
    live_ref, energy_ref, bprev_ref, vec, prev, tile, flipped, other, vt, vsrc, turned, tside, dpart, dsend, drecv, vch, tch, tout,
    row_out, rows_in,
    live_sem, energy_sem, bprev_sem, vec_sem, prev_sem, tile_sem,
    vd_send, vd_recv, vc_send, vc_recv, td_send, td_recv, tc_send, tc_recv,
    f_send, f_recv, dd_send, dd_recv, s_send, s_recv,
):
    nd = 2 * nt
    ny = nt // 4
    size = vec_ref.shape[0]
    share = vt.shape[1]
    me_p = lax.axis_index("diag")
    me_q = lax.axis_index("tile")
    z = lax.rem(me_p, nt)
    a = lax.div(me_p, nt)
    core = lax.rem(me_q, 2)
    chip = lax.div(me_q, 2)
    across = lax.rem(chip, 2)
    y = lax.div(chip, 2)
    v_nodes, v_sides = v_tree
    t_nodes, t_sides = t_tree

    load_vec = pltpu.make_async_copy(vec_ref, vec, vec_sem)
    load_vec.start()
    load_tile = pltpu.make_async_copy(tiles_ref.at[0, 0], tile, tile_sem)
    load_tile.start()
    load_prev = pltpu.make_async_copy(prev_ref, prev, prev_sem)
    load_prev.start()
    load_live = pltpu.make_async_copy(live_in, live_ref, live_sem)
    load_live.start()
    load_energy = pltpu.make_async_copy(energy_in, energy_ref, energy_sem)
    load_energy.start()
    load_bprev = pltpu.make_async_copy(bprev_in, bprev_ref, bprev_sem)
    load_bprev.start()

    def plane(shift):
        return nt * a + lax.rem(z + (shift + 2 * nt), nt)

    def dest(nodes, n, off):
        home = plane(-nodes[n][0])
        q = lax.rem(off + nt, nt)
        return lax.rem(home + q, nd), q

    def v_dest(n, off):
        p, q = dest(v_nodes, n, off)
        to = 2 * lax.div(q, 2) + core
        return p, q, to, jnp.logical_and(p == me_p, to == me_q)

    def node_plane(nodes, sides, q):
        seg = lax.rem(me_p - q + nd, nd)
        shift = jnp.int32(0)
        for n, offs in enumerate(sides):
            for off in offs:
                shift = shift + jnp.where(q == off % nt, nodes[n][0], 0)
        return nt * lax.div(seg, nt) + lax.rem(seg + shift + 2 * nt, nt)

    t_to = node_plane(t_nodes, t_sides, me_q)

    def chip_at(dy, db):
        row = lax.rem(y + dy + (ny - 2 * dy) * core + ny, ny)
        return 2 * row + lax.rem(across + db, 2)

    moves = [(dy, db) for dy, db in ORDER if dy < ny]
    spots = [(dy, db, dc) for dc in range(2) for dy, db in moves + [(0, 0)]]

    def tile_at(dy, db, dc):
        return 2 * chip_at(dy, db) + lax.rem(core + dc, 2)

    shifts = sorted(range(1, nt), key=lambda d: -min(d, nt - d)) + [0]
    others = [(da, dz) for dz in shifts for da in (1, 0) if (da, dz) != (0, 0)]

    def segment(da, dz):
        return nt * lax.rem(a + da, 2) + lax.rem(z + dz, nt)

    barrier = pltpu.get_barrier_semaphore()

    def greet(p, q):
        pl.semaphore_signal(barrier, inc=1, device_id=(p, q), device_id_type=MESH)

    expected = jnp.int32(0)

    def greet_unless(p, q, itself):
        @pl.when(jnp.logical_not(itself))
        def _():
            greet(p, q)

        return jnp.where(itself, 0, 1)

    def greet_chain(nodes):
        for off, parent in nodes:
            if parent is not None:
                step = off - nodes[parent][0]
                greet(plane(step), me_q)
                greet(plane(-step), me_q)
        return 2 * (len(nodes) - 1)

    expected = expected + greet_chain(v_nodes) + greet_chain(t_nodes)
    for n, offs in enumerate(v_sides):
        for off in offs:
            p, _, to, itself = v_dest(n, off)
            expected = expected + greet_unless(p, to, itself)
    for e in range(2):
        home = node_plane(v_nodes, v_sides, 2 * chip + e)
        for m in range(nt // 2):
            itself = jnp.logical_and(home == me_p, chip == m)
            expected = expected + greet_unless(home, 2 * m + core, itself)
    for n, offs in enumerate(t_sides):
        for off in offs:
            p, q = dest(t_nodes, n, off)
            itself = jnp.logical_and(p == me_p, q == me_q)
            expected = expected + greet_unless(p, q, itself)
    for j in range(nt):
        itself = jnp.logical_and(t_to == me_p, j == me_q)
        expected = expected + greet_unless(t_to, j, itself)
    for j in range(1, nt):
        greet(me_p, lax.rem(me_q + j, nt))
    greet(lax.rem(me_p + nt, nd), me_q)
    expected = expected + nt

    load_vec.wait()
    vt[...] = vec[...].T.reshape(nt, share, size)

    def remote(src, dst, send, recv, p, q):
        return pltpu.make_async_remote_copy(
            src_ref=src, dst_ref=dst, send_sem=send, recv_sem=recv,
            device_id=(p, q), device_id_type=MESH,
        )

    def arrived(ref, sem):
        pltpu.make_async_copy(ref, ref, sem).wait()

    v_cut, t_cut = ([pl.ds(i * size // n, size // n) for i in range(n)] for n in (V_PARTS, T_PARTS))

    def v_piece(n):
        return vt.at[me_q] if n == 0 else vch.at[n - 1]

    def v_hop(m, i):
        off, parent = v_nodes[m]
        return remote(
            v_piece(parent).at[:, v_cut[i]], vch.at[m - 1, :, v_cut[i]],
            vc_send.at[m - 1, i], vc_recv.at[m - 1, i],
            plane(off - v_nodes[parent][0]), me_q,
        )

    def v_forward(n, i):
        for m, (_, parent) in enumerate(v_nodes):
            if parent == n:
                v_hop(m, i).start()

    def v_out(n, off):
        p, q, to, itself = v_dest(n, off)
        e = lax.rem(q, 2)
        return (
            remote(v_piece(n), vsrc.at[e, chip], vd_send.at[q], vd_recv.at[e, chip], p, to),
            pltpu.make_async_copy(v_piece(n), vsrc.at[e, chip], vd_recv.at[e, chip]),
            itself,
        )

    def v_deliver(n):
        count = len(v_sides[n])
        for i in range(count):
            off = v_sides[n][0] + lax.rem(me_q + i, count)
            copy, stay, itself = v_out(n, off)

            @pl.when(itself)
            def _():
                stay.start()

            @pl.when(jnp.logical_not(itself))
            def _():
                copy.start()

    load_live.wait()
    live = live_ref[0, 0] * GROUP
    wide = 256 if size % 256 == 0 else 128

    def v_stage(n):
        for i, part in enumerate(v_cut):
            if n > 0:
                arrived(vch.at[n - 1, :, part], vc_recv.at[n - 1, i])
            v_forward(n, i)

    def t_product():
        flat = vt[...].reshape(nt * share, size)
        lanes = lax.broadcasted_iota(jnp.int32, flat.shape, 1)
        masked = jnp.where(lanes < live, flat, jnp.zeros_like(flat))
        load_tile.wait()

        @pl.loop(0, size // wide)
        def _(b):
            cols = pl.ds(pl.multiple_of(b * wide, wide), wide)
            prod = jnp.dot(masked, tile[:, cols], preferred_element_type=F32)
            turned[:, :, cols] = prod.astype(BF16).reshape(nt, share, wide)

    def f_swap():
        return remote(flipped, other, f_send, f_recv, me_p, me_q + 1 - 2 * core)

    def t_turn():
        @pl.loop(0, size // wide)
        def _(b):
            first = pl.multiple_of(b * wide, wide)
            part = pl.ds(first, wide)
            block = tile[part, :].T
            spot = lax.broadcasted_iota(jnp.int32, block.shape, 1) + first
            flipped[:, part] = jnp.where(spot < live, block, jnp.zeros_like(block))

        f_swap().start()

    def t_out(j):
        return remote(
            turned.at[j], tside.at[me_q], td_send.at[j], td_recv.at[me_q], t_to, j
        ), jnp.logical_and(t_to == me_p, j == me_q)

    def t_send(group):
        for spot in group:
            j = tile_at(*spot)
            copy, itself = t_out(j)

            @pl.when(itself)
            def _():
                pltpu.make_async_copy(turned.at[j], tside.at[me_q], td_recv.at[me_q]).start()

            @pl.when(jnp.logical_not(itself))
            def _():
                copy.start()

    def t_up(n, i):
        off, parent = t_nodes[n]
        return remote(
            tout.at[n - 1, :, t_cut[i]], tch.at[n - 1, :, t_cut[i]],
            tc_send.at[n - 1, i], tc_recv.at[n - 1, i],
            plane(t_nodes[parent][0] - off), me_q,
        )

    def t_sum(n, i):
        part = t_cut[i]
        total = None
        for off in t_sides[n]:
            if i == 0:
                arrived(tside.at[off % nt], td_recv.at[off % nt])
            piece = tside[off % nt, :, part].astype(F32)
            total = piece if total is None else total + piece
        for m, (_, parent) in enumerate(t_nodes):
            if parent == n:
                arrived(tch.at[m - 1, :, part], tc_recv.at[m - 1, i])
                total = total + tch[m - 1, :, part].astype(F32)
        return total

    def t_node(n):
        for i in range(T_PARTS):
            tout[n - 1, :, t_cut[i]] = t_sum(n, i).astype(BF16)
            t_up(n, i).start()

    half = nt * share // 2

    def d_product(second):
        e = 1 - core if second else core
        for m in range(nt // 2):
            arrived(vsrc.at[e, m], vd_recv.at[e, m])
        if second:
            arrived(other, f_recv)
        source = vsrc[e].reshape(half, size)

        @pl.loop(0, size // wide)
        def _(b):
            part = pl.ds(pl.multiple_of(b * wide, wide), wide)
            block = other[:, part] if second else flipped[:, part]
            prod = jnp.dot(source, block, preferred_element_type=F32).reshape(-1, share, wide)
            if second:
                prod = prod + dpart[:, :, part]
                dsend[:, :, part] = prod.astype(BF16)
            dpart[:, :, part] = prod

    def d_out(dy, db):
        m = chip_at(dy, db)
        return remote(
            dsend.at[m], drecv.at[chip], dd_send.at[m], dd_recv.at[chip], me_p, 2 * m + core
        ), m

    def d_share():
        for dy, db in moves:
            d_out(dy, db)[0].start()

    rank = jnp.int32(0)
    for n, offs in enumerate(t_sides):
        for off in offs:
            rank = rank + jnp.where(me_q == off % nt, min(abs(t_nodes[n][0]) // 3, 2), 0)
    at = [0, 0, 0]
    for word, number in PLAN if nt == 16 else SMALL:
        if word == "v":
            v_stage(number)
            v_deliver(number)
        elif word == "vf":
            v_stage(number)
        elif word == "vd":
            v_deliver(number)
        elif word == "greeted":
            pl.semaphore_wait(barrier, expected)
        elif word == "product":
            t_product()
        elif word == "turn":
            t_turn()
        elif word in ("near", "mid", "far"):
            k = ("near", "mid", "far").index(word)
            sent, at[k] = spots[at[k] : at[k] + number], at[k] + number

            @pl.when(rank == k)
            def _():
                t_send(sent)
        elif word == "node":
            t_node(number)
        elif word == "d":
            d_product(number)
        elif word == "share":
            d_share()

    line = lax.broadcasted_iota(jnp.int32, (share, 128), 0)
    lane = lax.broadcasted_iota(jnp.int32, (share, 128), 1)

    def as_row(column, slot):
        return jnp.sum(jnp.where(lane == line + slot * share, column, 0.0), axis=0, keepdims=True)

    def as_column(row):
        return jnp.sum(jnp.where(lane == line, row, 0.0), axis=1, keepdims=True)

    load_energy.wait()
    load_bprev.wait()
    load_prev.wait()
    square = [lax.broadcasted_iota(jnp.int32, (share, share), d) for d in range(2)]
    before = jnp.where(square[0] == square[1], bprev_ref[...].reshape(1, share), 0.0)
    before = jnp.sum(before, axis=1, keepdims=True)
    own = vt[me_q].astype(F32)
    diagonal = energy_ref[...].reshape(1, size) * own
    behind = before * prev[...]
    norm = jnp.sum(own * own, axis=1, keepdims=True)
    back = jnp.sum(own * behind, axis=1, keepdims=True)

    total = jnp.concatenate([t_sum(0, i) for i in range(T_PARTS)], axis=1)
    total = total + dpart[chip]
    for dy, db in moves:
        m = chip_at(dy, db)
        arrived(drecv.at[m], dd_recv.at[m])
        total = total + drecv[m].astype(F32)

    hv = total + diagonal
    w = hv - behind
    numer = jnp.sum(own * hv, axis=1, keepdims=True)
    slope = (numer - back) / jnp.where(norm > 0.0, norm, 1.0)
    rest = w - slope * own
    rest = jnp.sum(rest * rest, axis=1, keepdims=True)
    row_out[0] = as_row(numer, 0) + as_row(norm, 1) + as_row(slope, 2) + as_row(rest, 3)
    for da, dz in others:
        remote(row_out.at[0], rows_in.at[me_p], s_send, s_recv, segment(da, dz), me_q).start()
    rows_in[me_p] = row_out[0]
    arrived(rows_in.at[pl.ds(0, nd - 1)], s_recv)

    rows = rows_in[...].reshape(nd, 128)
    norms = pltpu.roll(rows, 128 - share, 1)
    slopes = pltpu.roll(rows, 128 - 2 * share, 1)
    rests = pltpu.roll(rows, 128 - 3 * share, 1)
    alpha = jnp.sum(rows, axis=0, keepdims=True) / jnp.sum(norms, axis=0, keepdims=True)
    gap = slopes - alpha
    squared = jnp.sum(rests + gap * norms * gap, axis=0, keepdims=True)
    beta = jnp.sqrt(squared / rows_total + 1e-06)
    alpha_ref[...] = alpha
    beta_ref[...] = beta
    out_ref[...] = (w - as_column(alpha) * own) / as_column(beta)

    for n in range(len(v_nodes)):
        for off in v_sides[n]:
            copy, _, itself = v_out(n, off)

            @pl.when(jnp.logical_not(itself))
            def _():
                copy.wait_send()

        if n > 0:
            for i in range(V_PARTS):
                v_hop(n, i).wait_send()
    for n in range(1, len(t_nodes)):
        for i in range(T_PARTS):
            t_up(n, i).wait_send()
    for j in range(nt):
        copy, itself = t_out(j)

        @pl.when(jnp.logical_not(itself))
        def _():
            copy.wait_send()

    f_swap().wait_send()
    for dy, db in moves:
        d_out(dy, db)[0].wait_send()
    arrived(rows_in.at[pl.ds(0, nd - 1)], s_send)


def body(tiles, live_groups, vectors, previous, energies, beta_prev):
    nt = lax.axis_size("tile")
    nd = lax.axis_size("diag")
    size, columns = vectors.shape
    share = columns // nt
    v_tree, t_tree = trees_of(nt)
    v_more, t_more = max(len(v_tree[0]) - 1, 1), max(len(t_tree[0]) - 1, 1)
    vmem = pl.BlockSpec(memory_space=pltpu.VMEM)
    hbm = pl.BlockSpec(memory_space=pl.ANY)
    dma = pltpu.SemaphoreType.DMA
    out, alpha, beta = pl.pallas_call(
        functools.partial(kernel, nt, v_tree, t_tree, float(size * nd)),
        out_shape=(
            jax.ShapeDtypeStruct((share, size), F32),
            jax.ShapeDtypeStruct((1, 128), F32),
            jax.ShapeDtypeStruct((1, 128), F32),
        ),
        in_specs=[hbm] * 6,
        out_specs=(vmem, vmem, vmem),
        scratch_shapes=[
            pltpu.SMEM((1, 1), jnp.int32),
            pltpu.VMEM((size,), F32),
            pltpu.VMEM((share,), F32),
            pltpu.VMEM((size, columns), BF16),
            pltpu.VMEM((share, size), F32),
            pltpu.VMEM((size, size), BF16),
            pltpu.VMEM((size, size), BF16),
            pltpu.VMEM((size, size), BF16),
            pltpu.VMEM((nt, share, size), BF16),
            pltpu.VMEM((2, nt // 2, share, size), BF16),
            pltpu.VMEM((nt, share, size), BF16),
            pltpu.VMEM((nt, share, size), BF16),
            pltpu.VMEM((nt // 2, share, size), F32),
            pltpu.VMEM((nt // 2, share, size), BF16),
            pltpu.VMEM((nt // 2, share, size), BF16),
            pltpu.VMEM((v_more, share, size), BF16),
            pltpu.VMEM((t_more, share, size), BF16),
            pltpu.VMEM((t_more, share, size), BF16),
            pltpu.VMEM((1, 1, 128), F32),
            pltpu.VMEM((nd, 1, 128), F32),
            dma, dma, dma, dma, dma, dma,
            dma((nt,)), dma((2, nt // 2)), dma((v_more, V_PARTS)), dma((v_more, V_PARTS)),
            dma((nt,)), dma((nt,)), dma((t_more, T_PARTS)), dma((t_more, T_PARTS)),
            dma, dma, dma((nt // 2,)), dma((nt // 2,)),
            dma, dma,
        ],
        compiler_params=pltpu.CompilerParams(
            collective_id=0, has_side_effects=True, vmem_limit_bytes=VMEM_MIB * 1024 * 1024
        ),
    )(live_groups, energies, beta_prev, vectors, previous.T, tiles)
    return out.T, alpha[0, :share], beta[0, :share]


def solution(mesh):
    return jax.shard_map(
        body,
        mesh=mesh,
        in_specs=(
            P("diag", "tile", None, None),
            P("diag", "tile"),
            P("diag", None),
            P("diag", "tile"),
            P("diag"),
            P("tile"),
        ),
        out_specs=(P("diag", "tile"), P("tile"), P("tile")),
        check_vma=False,
    )
```

```python
import functools

import jax
import jax.numpy as jnp
from jax import lax
from jax.experimental import pallas as pl
from jax.experimental.pallas import tpu as pltpu
from jax.sharding import PartitionSpec as P

GROUP = 128
MESH = pl.DeviceIdType.MESH
F32 = jnp.float32
BF16 = jnp.bfloat16
ORDER = ((1, 0), (3, 0), (0, 1), (2, 0), (1, 1), (3, 1), (2, 1))
VMEM_MIB = 58
V_PARTS = 1
T_PARTS = 1
PLAN = (('product', 0), ('greeted', 0), ('v', 0), ('far', 8), ('mid', 8), ('near', 8), ('turn', 0), ('v', 1), ('v', 2), ('far', 8), ('mid', 8), ('near', 8), ('v', 3), ('v', 4), ('node', 5), ('node', 3), ('node', 4), ('d', 0), ('d', 1), ('node', 1), ('node', 2))
SMALL = (("greeted", 0), ("v", 0), ("product", 0), ("near", 2), ("v", 1), ("turn", 0), ("v", 2), ("near", 2), ("node", 2), ("node", 1), ("d", 0), ("d", 1), ("share", 0))


def offsets_of(nt):
    return range(-(nt // 2) + 1, nt // 2 + 1)


def tree_of(nt, nodes):
    sides = [[] for _ in nodes]
    for off in offsets_of(nt):
        best = min(range(len(nodes)), key=lambda n: (abs(nodes[n][0] - off), n))
        sides[best].append(off)
    return nodes, sides


def trees_of(nt):
    if nt == 16:
        chain = [(0, None), (3, 0), (-3, 0), (6, 1), (-6, 2)]
        return tree_of(nt, chain), tree_of(nt, chain + [(8, 3)])
    if nt == 4:
        return tree_of(nt, [(0, None), (1, 0), (2, 1)]), tree_of(nt, [(0, None), (1, 0), (2, 1)])
    return tree_of(nt, [(0, None)]), tree_of(nt, [(0, None)])


def kernel(
    nt, v_tree, t_tree, rows_total,
    live_in, energy_in, bprev_in, vec_ref, prev_ref, tiles_ref,
    out_ref, alpha_ref, beta_ref,
    live_ref, energy_ref, bprev_ref, vec, prev, tile, flipped, other, vt, vsrc, turned, tside, dpart, dsend, drecv, vch, tch, tout,
    row_out, rows_in,
    live_sem, energy_sem, bprev_sem, vec_sem, prev_sem, tile_sem,
    vd_send, vd_recv, vc_send, vc_recv, td_send, td_recv, tc_send, tc_recv,
    f_send, f_recv, dd_send, dd_recv, s_send, s_recv,
):
    nd = 2 * nt
    ny = nt // 4
    size = vec_ref.shape[0]
    share = vt.shape[1]
    me_p = lax.axis_index("diag")
    me_q = lax.axis_index("tile")
    z = lax.rem(me_p, nt)
    a = lax.div(me_p, nt)
    core = lax.rem(me_q, 2)
    chip = lax.div(me_q, 2)
    across = lax.rem(chip, 2)
    y = lax.div(chip, 2)
    v_nodes, v_sides = v_tree
    t_nodes, t_sides = t_tree

    load_vec = pltpu.make_async_copy(vec_ref, vec, vec_sem)
    load_vec.start()
    load_tile = pltpu.make_async_copy(tiles_ref.at[0, 0], tile, tile_sem)
    load_tile.start()
    load_prev = pltpu.make_async_copy(prev_ref, prev, prev_sem)
    load_prev.start()
    load_live = pltpu.make_async_copy(live_in, live_ref, live_sem)
    load_live.start()
    load_energy = pltpu.make_async_copy(energy_in, energy_ref, energy_sem)
    load_energy.start()
    load_bprev = pltpu.make_async_copy(bprev_in, bprev_ref, bprev_sem)
    load_bprev.start()

    def plane(shift):
        return nt * a + lax.rem(z + (shift + 2 * nt), nt)

    def dest(nodes, n, off):
        home = plane(-nodes[n][0])
        q = lax.rem(off + nt, nt)
        return lax.rem(home + q, nd), q

    def v_dest(n, off):
        p, q = dest(v_nodes, n, off)
        to = 2 * lax.div(q, 2) + core
        return p, q, to, jnp.logical_and(p == me_p, to == me_q)

    def node_plane(nodes, sides, q):
        seg = lax.rem(me_p - q + nd, nd)
        shift = jnp.int32(0)
        for n, offs in enumerate(sides):
            for off in offs:
                shift = shift + jnp.where(q == off % nt, nodes[n][0], 0)
        return nt * lax.div(seg, nt) + lax.rem(seg + shift + 2 * nt, nt)

    t_to = node_plane(t_nodes, t_sides, me_q)

    def chip_at(dy, db):
        row = lax.rem(y + dy, ny)
        return 2 * row + lax.rem(across + db, 2)

    moves = [(dy, db) for dy, db in ORDER if dy < ny]
    spots = [(dy, db, dc) for dc in range(2) for dy, db in moves + [(0, 0)]]

    def tile_at(dy, db, dc):
        return 2 * chip_at(dy, db) + lax.rem(core + dc, 2)

    shifts = sorted(range(1, nt), key=lambda d: -min(d, nt - d)) + [0]
    others = [(da, dz) for dz in shifts for da in (1, 0) if (da, dz) != (0, 0)]

    def segment(da, dz):
        return nt * lax.rem(a + da, 2) + lax.rem(z + dz, nt)

    barrier = pltpu.get_barrier_semaphore()

    def greet(p, q):
        pl.semaphore_signal(barrier, inc=1, device_id=(p, q), device_id_type=MESH)

    expected = jnp.int32(0)

    def greet_unless(p, q, itself):
        @pl.when(jnp.logical_not(itself))
        def _():
            greet(p, q)

        return jnp.where(itself, 0, 1)

    def greet_chain(nodes):
        for off, parent in nodes:
            if parent is not None:
                step = off - nodes[parent][0]
                greet(plane(step), me_q)
                greet(plane(-step), me_q)
        return 2 * (len(nodes) - 1)

    expected = expected + greet_chain(v_nodes) + greet_chain(t_nodes)
    for n, offs in enumerate(v_sides):
        for off in offs:
            p, _, to, itself = v_dest(n, off)
            expected = expected + greet_unless(p, to, itself)
    for e in range(2):
        home = node_plane(v_nodes, v_sides, 2 * chip + e)
        for m in range(nt // 2):
            itself = jnp.logical_and(home == me_p, chip == m)
            expected = expected + greet_unless(home, 2 * m + core, itself)
    for n, offs in enumerate(t_sides):
        for off in offs:
            p, q = dest(t_nodes, n, off)
            itself = jnp.logical_and(p == me_p, q == me_q)
            expected = expected + greet_unless(p, q, itself)
    for j in range(nt):
        itself = jnp.logical_and(t_to == me_p, j == me_q)
        expected = expected + greet_unless(t_to, j, itself)
    for j in range(1, nt):
        greet(me_p, lax.rem(me_q + j, nt))
    greet(lax.rem(me_p + nt, nd), me_q)
    expected = expected + nt

    load_vec.wait()
    vt[...] = vec[...].T.reshape(nt, share, size)

    def remote(src, dst, send, recv, p, q):
        return pltpu.make_async_remote_copy(
            src_ref=src, dst_ref=dst, send_sem=send, recv_sem=recv,
            device_id=(p, q), device_id_type=MESH,
        )

    def arrived(ref, sem):
        pltpu.make_async_copy(ref, ref, sem).wait()

    v_cut, t_cut = ([pl.ds(i * size // n, size // n) for i in range(n)] for n in (V_PARTS, T_PARTS))

    def v_piece(n):
        return vt.at[me_q] if n == 0 else vch.at[n - 1]

    def v_hop(m, i):
        off, parent = v_nodes[m]
        return remote(
            v_piece(parent).at[:, v_cut[i]], vch.at[m - 1, :, v_cut[i]],
            vc_send.at[m - 1, i], vc_recv.at[m - 1, i],
            plane(off - v_nodes[parent][0]), me_q,
        )

    def v_forward(n, i):
        for m, (_, parent) in enumerate(v_nodes):
            if parent == n:
                v_hop(m, i).start()

    def v_out(n, off):
        p, q, to, itself = v_dest(n, off)
        e = lax.rem(q, 2)
        return (
            remote(v_piece(n), vsrc.at[e, chip], vd_send.at[q], vd_recv.at[e, chip], p, to),
            pltpu.make_async_copy(v_piece(n), vsrc.at[e, chip], vd_recv.at[e, chip]),
            itself,
        )

    def v_deliver(n):
        count = len(v_sides[n])
        for i in range(count):
            off = v_sides[n][0] + lax.rem(me_q + i, count)
            copy, stay, itself = v_out(n, off)

            @pl.when(itself)
            def _():
                stay.start()

            @pl.when(jnp.logical_not(itself))
            def _():
                copy.start()

    load_live.wait()
    live = live_ref[0, 0] * GROUP
    wide = 256 if size % 256 == 0 else 128

    def v_stage(n):
        for i, part in enumerate(v_cut):
            if n > 0:
                arrived(vch.at[n - 1, :, part], vc_recv.at[n - 1, i])
            v_forward(n, i)

    def t_product():
        flat = vt[...].reshape(nt * share, size)
        lanes = lax.broadcasted_iota(jnp.int32, flat.shape, 1)
        masked = jnp.where(lanes < live, flat, jnp.zeros_like(flat))
        load_tile.wait()

        @pl.loop(0, size // wide)
        def _(b):
            cols = pl.ds(pl.multiple_of(b * wide, wide), wide)
            prod = jnp.dot(masked, tile[:, cols], preferred_element_type=F32)
            turned[:, :, cols] = prod.astype(BF16).reshape(nt, share, wide)

    def f_swap():
        return remote(flipped, other, f_send, f_recv, me_p, me_q + 1 - 2 * core)

    def t_turn():
        @pl.loop(0, size // wide)
        def _(b):
            first = pl.multiple_of(b * wide, wide)
            part = pl.ds(first, wide)
            block = tile[part, :].T
            spot = lax.broadcasted_iota(jnp.int32, block.shape, 1) + first
            flipped[:, part] = jnp.where(spot < live, block, jnp.zeros_like(block))

        f_swap().start()

    def t_out(j):
        return remote(
            turned.at[j], tside.at[me_q], td_send.at[j], td_recv.at[me_q], t_to, j
        ), jnp.logical_and(t_to == me_p, j == me_q)

    def t_send(group):
        for spot in group:
            j = tile_at(*spot)
            copy, itself = t_out(j)

            @pl.when(itself)
            def _():
                pltpu.make_async_copy(turned.at[j], tside.at[me_q], td_recv.at[me_q]).start()

            @pl.when(jnp.logical_not(itself))
            def _():
                copy.start()

    def t_up(n, i):
        off, parent = t_nodes[n]
        return remote(
            tout.at[n - 1, :, t_cut[i]], tch.at[n - 1, :, t_cut[i]],
            tc_send.at[n - 1, i], tc_recv.at[n - 1, i],
            plane(t_nodes[parent][0] - off), me_q,
        )

    def t_sum(n, i):
        part = t_cut[i]
        total = None
        for off in t_sides[n]:
            if i == 0:
                arrived(tside.at[off % nt], td_recv.at[off % nt])
            piece = tside[off % nt, :, part].astype(F32)
            total = piece if total is None else total + piece
        for m, (_, parent) in enumerate(t_nodes):
            if parent == n:
                arrived(tch.at[m - 1, :, part], tc_recv.at[m - 1, i])
                total = total + tch[m - 1, :, part].astype(F32)
        return total

    def t_node(n):
        for i in range(T_PARTS):
            tout[n - 1, :, t_cut[i]] = t_sum(n, i).astype(BF16)
            t_up(n, i).start()

    blocks = size // wide
    d_cut = [(0, blocks - blocks // 2), (blocks - blocks // 2, blocks)][: min(blocks, 2)]

    def d_part(i):
        return pl.ds(d_cut[i][0] * wide, (d_cut[i][1] - d_cut[i][0]) * wide)

    def d_out(dy, db, i):
        m = chip_at(dy, db)
        return remote(
            dsend.at[m, :, d_part(i)], drecv.at[chip, :, d_part(i)],
            dd_send.at[m, i], dd_recv.at[chip, i], me_p, 2 * m + core,
        )

    def d_share(i):
        for dy, db in moves:
            d_out(dy, db, i).start()

    half = nt * share // 2

    def d_product(second):
        e = 1 - core if second else core
        for m in range(nt // 2):
            arrived(vsrc.at[e, m], vd_recv.at[e, m])
        if second:
            arrived(other, f_recv)
        source = vsrc[e].reshape(half, size)

        def columns(b):
            part = pl.ds(pl.multiple_of(b * wide, wide), wide)
            block = other[:, part] if second else flipped[:, part]
            prod = jnp.dot(source, block, preferred_element_type=F32).reshape(-1, share, wide)
            if second:
                prod = prod + dpart[:, :, part]
                dsend[:, :, part] = prod.astype(BF16)
            dpart[:, :, part] = prod

        if second:
            for i, (first, last) in enumerate(d_cut):
                pl.loop(first, last)(columns)
                d_share(i)
        else:
            pl.loop(0, size // wide)(columns)

    rank = jnp.int32(0)
    for n, offs in enumerate(t_sides):
        for off in offs:
            rank = rank + jnp.where(me_q == off % nt, min(abs(t_nodes[n][0]) // 3, 2), 0)
    at = [0, 0, 0]
    for word, number in PLAN if nt == 16 else SMALL:
        if word == "v":
            v_stage(number)
            v_deliver(number)
        elif word == "vf":
            v_stage(number)
        elif word == "vd":
            v_deliver(number)
        elif word == "greeted":
            pl.semaphore_wait(barrier, expected)
        elif word == "product":
            t_product()
        elif word == "turn":
            t_turn()
        elif word in ("near", "mid", "far"):
            k = ("near", "mid", "far").index(word)
            sent, at[k] = spots[at[k] : at[k] + number], at[k] + number

            @pl.when(rank == k)
            def _():
                t_send(sent)
        elif word == "node":
            t_node(number)
        elif word == "d":
            d_product(number)

    line = lax.broadcasted_iota(jnp.int32, (share, 128), 0)
    lane = lax.broadcasted_iota(jnp.int32, (share, 128), 1)

    def as_row(column, slot):
        return jnp.sum(jnp.where(lane == line + slot * share, column, 0.0), axis=0, keepdims=True)

    def as_column(row):
        return jnp.sum(jnp.where(lane == line, row, 0.0), axis=1, keepdims=True)

    load_energy.wait()
    load_bprev.wait()
    load_prev.wait()
    square = [lax.broadcasted_iota(jnp.int32, (share, share), d) for d in range(2)]
    before = jnp.where(square[0] == square[1], bprev_ref[...].reshape(1, share), 0.0)
    before = jnp.sum(before, axis=1, keepdims=True)
    own = vt[me_q].astype(F32)
    diagonal = energy_ref[...].reshape(1, size) * own
    behind = before * prev[...]
    norm = jnp.sum(own * own, axis=1, keepdims=True)
    back = jnp.sum(own * behind, axis=1, keepdims=True)

    total = jnp.concatenate([t_sum(0, i) for i in range(T_PARTS)], axis=1)
    total = total + dpart[chip]
    for dy, db in moves:
        m = chip_at(dy, db)
        for i in range(len(d_cut)):
            arrived(drecv.at[m, :, d_part(i)], dd_recv.at[m, i])
        total = total + drecv[m].astype(F32)

    hv = total + diagonal
    w = hv - behind
    numer = jnp.sum(own * hv, axis=1, keepdims=True)
    slope = (numer - back) / jnp.where(norm > 0.0, norm, 1.0)
    rest = w - slope * own
    rest = jnp.sum(rest * rest, axis=1, keepdims=True)
    row_out[0] = as_row(numer, 0) + as_row(norm, 1) + as_row(slope, 2) + as_row(rest, 3)
    for da, dz in others:
        remote(row_out.at[0], rows_in.at[me_p], s_send, s_recv, segment(da, dz), me_q).start()
    rows_in[me_p] = row_out[0]
    arrived(rows_in.at[pl.ds(0, nd - 1)], s_recv)

    rows = rows_in[...].reshape(nd, 128)
    norms = pltpu.roll(rows, 128 - share, 1)
    slopes = pltpu.roll(rows, 128 - 2 * share, 1)
    rests = pltpu.roll(rows, 128 - 3 * share, 1)
    alpha = jnp.sum(rows, axis=0, keepdims=True) / jnp.sum(norms, axis=0, keepdims=True)
    gap = slopes - alpha
    squared = jnp.sum(rests + gap * norms * gap, axis=0, keepdims=True)
    beta = jnp.sqrt(squared / rows_total + 1e-06)
    alpha_ref[...] = alpha
    beta_ref[...] = beta
    out_ref[...] = (w - as_column(alpha) * own) / as_column(beta)

    for n in range(len(v_nodes)):
        for off in v_sides[n]:
            copy, _, itself = v_out(n, off)

            @pl.when(jnp.logical_not(itself))
            def _():
                copy.wait_send()

        if n > 0:
            for i in range(V_PARTS):
                v_hop(n, i).wait_send()
    for n in range(1, len(t_nodes)):
        for i in range(T_PARTS):
            t_up(n, i).wait_send()
    for j in range(nt):
        copy, itself = t_out(j)

        @pl.when(jnp.logical_not(itself))
        def _():
            copy.wait_send()

    f_swap().wait_send()
    for dy, db in moves:
        for i in range(len(d_cut)):
            d_out(dy, db, i).wait_send()
    arrived(rows_in.at[pl.ds(0, nd - 1)], s_send)


def body(tiles, live_groups, vectors, previous, energies, beta_prev):
    nt = lax.axis_size("tile")
    nd = lax.axis_size("diag")
    size, columns = vectors.shape
    share = columns // nt
    v_tree, t_tree = trees_of(nt)
    v_more, t_more = max(len(v_tree[0]) - 1, 1), max(len(t_tree[0]) - 1, 1)
    vmem = pl.BlockSpec(memory_space=pltpu.VMEM)
    hbm = pl.BlockSpec(memory_space=pl.ANY)
    dma = pltpu.SemaphoreType.DMA
    out, alpha, beta = pl.pallas_call(
        functools.partial(kernel, nt, v_tree, t_tree, float(size * nd)),
        out_shape=(
            jax.ShapeDtypeStruct((share, size), F32),
            jax.ShapeDtypeStruct((1, 128), F32),
            jax.ShapeDtypeStruct((1, 128), F32),
        ),
        in_specs=[hbm] * 6,
        out_specs=(vmem, vmem, vmem),
        scratch_shapes=[
            pltpu.SMEM((1, 1), jnp.int32),
            pltpu.VMEM((size,), F32),
            pltpu.VMEM((share,), F32),
            pltpu.VMEM((size, columns), BF16),
            pltpu.VMEM((share, size), F32),
            pltpu.VMEM((size, size), BF16),
            pltpu.VMEM((size, size), BF16),
            pltpu.VMEM((size, size), BF16),
            pltpu.VMEM((nt, share, size), BF16),
            pltpu.VMEM((2, nt // 2, share, size), BF16),
            pltpu.VMEM((nt, share, size), BF16),
            pltpu.VMEM((nt, share, size), BF16),
            pltpu.VMEM((nt // 2, share, size), F32),
            pltpu.VMEM((nt // 2, share, size), BF16),
            pltpu.VMEM((nt // 2, share, size), BF16),
            pltpu.VMEM((v_more, share, size), BF16),
            pltpu.VMEM((t_more, share, size), BF16),
            pltpu.VMEM((t_more, share, size), BF16),
            pltpu.VMEM((1, 1, 128), F32),
            pltpu.VMEM((nd, 1, 128), F32),
            dma, dma, dma, dma, dma, dma,
            dma((nt,)), dma((2, nt // 2)), dma((v_more, V_PARTS)), dma((v_more, V_PARTS)),
            dma((nt,)), dma((nt,)), dma((t_more, T_PARTS)), dma((t_more, T_PARTS)),
            dma, dma, dma((nt // 2, 2)), dma((nt // 2, 2)),
            dma, dma,
        ],
        compiler_params=pltpu.CompilerParams(
            collective_id=0, has_side_effects=True, vmem_limit_bytes=VMEM_MIB * 1024 * 1024
        ),
    )(live_groups, energies, beta_prev, vectors, previous.T, tiles)
    return out.T, alpha[0, :share], beta[0, :share]


def solution(mesh):
    return jax.shard_map(
        body,
        mesh=mesh,
        in_specs=(
            P("diag", "tile", None, None),
            P("diag", "tile"),
            P("diag", None),
            P("diag", "tile"),
            P("diag"),
            P("tile"),
        ),
        out_specs=(P("diag", "tile"), P("tile"), P("tile")),
        check_vma=False,
    )
```

```python
import functools

import jax
import jax.numpy as jnp
from jax import lax
from jax.experimental import pallas as pl
from jax.experimental.pallas import tpu as pltpu
from jax.sharding import PartitionSpec as P

GROUP = 128
MESH = pl.DeviceIdType.MESH
F32 = jnp.float32
BF16 = jnp.bfloat16
ORDER = ((1, 0), (3, 0), (0, 1), (1, 1), (3, 1), (2, 0), (2, 1))
VMEM_KIB = 54784
V_PARTS = 1
T_PARTS = 2
PLAN = (('product', 0), ('greeted', 0), ('v', 0), ('far', 8), ('mid', 8), ('near', 8), ('turn', 0), ('v', 1), ('v', 2), ('far', 8), ('mid', 8), ('near', 8), ('v', 3), ('v', 4), ('node', 5), ('node', 3), ('node', 4), ('d', 0), ('d', 1), ('node', 1), ('node', 2))
SMALL = (("greeted", 0), ("v", 0), ("product", 0), ("near", 2), ("v", 1), ("turn", 0), ("v", 2), ("near", 2), ("node", 2), ("node", 1), ("d", 0), ("d", 1), ("share", 0))


def offsets_of(nt):
    return range(-(nt // 2) + 1, nt // 2 + 1)


def tree_of(nt, nodes):
    sides = [[] for _ in nodes]
    for off in offsets_of(nt):
        best = min(range(len(nodes)), key=lambda n: (abs(nodes[n][0] - off), n))
        sides[best].append(off)
    return nodes, sides


def trees_of(nt):
    if nt == 16:
        chain = [(0, None), (3, 0), (-3, 0), (6, 1), (-6, 2)]
        return tree_of(nt, chain), tree_of(nt, chain + [(8, 3)])
    if nt == 4:
        return tree_of(nt, [(0, None), (1, 0), (2, 1)]), tree_of(nt, [(0, None), (1, 0), (2, 1)])
    return tree_of(nt, [(0, None)]), tree_of(nt, [(0, None)])


def kernel(
    nt, v_tree, t_tree, rows_total,
    live_in, energy_in, bprev_in, vec_ref, prev_ref, tiles_ref,
    out_ref, alpha_ref, beta_ref,
    live_ref, energy_ref, bprev_ref, vec, prev, tile, flipped, other, vt, vsrc, turned, tside, dpart, dsend, drecv, vch, tch, tout,
    row_out, rows_in,
    live_sem, energy_sem, bprev_sem, vec_sem, prev_sem, tile_sem,
    vd_send, vd_recv, vc_send, vc_recv, td_send, td_recv, tc_send, tc_recv,
    f_send, f_recv, dd_send, dd_recv, s_send, s_recv,
):
    nd = 2 * nt
    ny = nt // 4
    size = vec_ref.shape[0]
    share = vt.shape[1]
    me_p = lax.axis_index("diag")
    me_q = lax.axis_index("tile")
    z = lax.rem(me_p, nt)
    a = lax.div(me_p, nt)
    core = lax.rem(me_q, 2)
    chip = lax.div(me_q, 2)
    across = lax.rem(chip, 2)
    y = lax.div(chip, 2)
    v_nodes, v_sides = v_tree
    t_nodes, t_sides = t_tree

    load_vec = pltpu.make_async_copy(vec_ref, vec, vec_sem)
    load_vec.start()
    load_tile = pltpu.make_async_copy(tiles_ref.at[0, 0], tile, tile_sem)
    load_tile.start()
    load_prev = pltpu.make_async_copy(prev_ref, prev, prev_sem)
    load_prev.start()
    load_live = pltpu.make_async_copy(live_in, live_ref, live_sem)
    load_live.start()
    load_energy = pltpu.make_async_copy(energy_in, energy_ref, energy_sem)
    load_energy.start()
    load_bprev = pltpu.make_async_copy(bprev_in, bprev_ref, bprev_sem)
    load_bprev.start()

    def plane(shift):
        return nt * a + lax.rem(z + (shift + 2 * nt), nt)

    def dest(nodes, n, off):
        home = plane(-nodes[n][0])
        q = lax.rem(off + nt, nt)
        return lax.rem(home + q, nd), q

    def v_dest(n, off):
        p, q = dest(v_nodes, n, off)
        to = 2 * lax.div(q, 2) + core
        return p, q, to, jnp.logical_and(p == me_p, to == me_q)

    def node_plane(nodes, sides, q):
        seg = lax.rem(me_p - q + nd, nd)
        shift = jnp.int32(0)
        for n, offs in enumerate(sides):
            for off in offs:
                shift = shift + jnp.where(q == off % nt, nodes[n][0], 0)
        return nt * lax.div(seg, nt) + lax.rem(seg + shift + 2 * nt, nt)

    t_to = node_plane(t_nodes, t_sides, me_q)

    def chip_at(dy, db):
        row = lax.rem(y + dy, ny)
        return 2 * row + lax.rem(across + db, 2)

    moves = [(dy, db) for dy, db in ORDER if dy < ny]
    spots = [(dy, db, dc) for dc in range(2) for dy, db in moves + [(0, 0)]]

    def tile_at(dy, db, dc):
        return 2 * chip_at(dy, db) + lax.rem(core + dc, 2)

    shifts = sorted(range(1, nt), key=lambda d: -min(d, nt - d)) + [0]
    others = [(da, dz) for dz in shifts for da in (1, 0) if (da, dz) != (0, 0)]

    def segment(da, dz):
        return nt * lax.rem(a + da, 2) + lax.rem(z + dz, nt)

    barrier = pltpu.get_barrier_semaphore()

    def greet(p, q):
        pl.semaphore_signal(barrier, inc=1, device_id=(p, q), device_id_type=MESH)

    expected = jnp.int32(0)

    def greet_unless(p, q, itself):
        @pl.when(jnp.logical_not(itself))
        def _():
            greet(p, q)

        return jnp.where(itself, 0, 1)

    def greet_chain(nodes):
        for off, parent in nodes:
            if parent is not None:
                step = off - nodes[parent][0]
                greet(plane(step), me_q)
                greet(plane(-step), me_q)
        return 2 * (len(nodes) - 1)

    expected = expected + greet_chain(v_nodes) + greet_chain(t_nodes)
    for n, offs in enumerate(v_sides):
        for off in offs:
            p, _, to, itself = v_dest(n, off)
            expected = expected + greet_unless(p, to, itself)
    for e in range(2):
        home = node_plane(v_nodes, v_sides, 2 * chip + e)
        for m in range(nt // 2):
            itself = jnp.logical_and(home == me_p, chip == m)
            expected = expected + greet_unless(home, 2 * m + core, itself)
    for n, offs in enumerate(t_sides):
        for off in offs:
            p, q = dest(t_nodes, n, off)
            itself = jnp.logical_and(p == me_p, q == me_q)
            expected = expected + greet_unless(p, q, itself)
    for j in range(nt):
        itself = jnp.logical_and(t_to == me_p, j == me_q)
        expected = expected + greet_unless(t_to, j, itself)
    for j in range(1, nt):
        greet(me_p, lax.rem(me_q + j, nt))
    greet(lax.rem(me_p + nt, nd), me_q)
    expected = expected + nt

    load_vec.wait()
    vt[...] = vec[...].T.reshape(nt, share, size)

    def remote(src, dst, send, recv, p, q):
        return pltpu.make_async_remote_copy(
            src_ref=src, dst_ref=dst, send_sem=send, recv_sem=recv,
            device_id=(p, q), device_id_type=MESH,
        )

    def arrived(ref, sem):
        pltpu.make_async_copy(ref, ref, sem).wait()

    v_cut, t_cut = ([pl.ds(i * size // n, size // n) for i in range(n)] for n in (V_PARTS, T_PARTS))

    def v_piece(n):
        return vt.at[me_q] if n == 0 else vch.at[n - 1]

    def v_hop(m, i):
        off, parent = v_nodes[m]
        return remote(
            v_piece(parent).at[:, v_cut[i]], vch.at[m - 1, :, v_cut[i]],
            vc_send.at[m - 1, i], vc_recv.at[m - 1, i],
            plane(off - v_nodes[parent][0]), me_q,
        )

    def v_forward(n, i):
        for m, (_, parent) in enumerate(v_nodes):
            if parent == n:
                v_hop(m, i).start()

    def v_out(n, off):
        p, q, to, itself = v_dest(n, off)
        e = lax.rem(q, 2)
        return (
            remote(v_piece(n), vsrc.at[e, chip], vd_send.at[q], vd_recv.at[e, chip], p, to),
            pltpu.make_async_copy(v_piece(n), vsrc.at[e, chip], vd_recv.at[e, chip]),
            itself,
        )

    def v_deliver(n):
        count = len(v_sides[n])
        for i in range(count):
            off = v_sides[n][0] + lax.rem(me_q + i, count)
            copy, stay, itself = v_out(n, off)

            @pl.when(itself)
            def _():
                stay.start()

            @pl.when(jnp.logical_not(itself))
            def _():
                copy.start()

    load_live.wait()
    live = live_ref[0, 0] * GROUP
    wide = 256 if size % 256 == 0 else 128

    def v_stage(n):
        for i, part in enumerate(v_cut):
            if n > 0:
                arrived(vch.at[n - 1, :, part], vc_recv.at[n - 1, i])
            v_forward(n, i)

    def t_product():
        flat = vt[...].reshape(nt * share, size)
        lanes = lax.broadcasted_iota(jnp.int32, flat.shape, 1)
        masked = jnp.where(lanes < live, flat, jnp.zeros_like(flat))
        load_tile.wait()

        @pl.loop(0, size // wide)
        def _(b):
            cols = pl.ds(pl.multiple_of(b * wide, wide), wide)
            prod = jnp.dot(masked, tile[:, cols], preferred_element_type=F32)
            turned[:, :, cols] = prod.astype(BF16).reshape(nt, share, wide)

    def f_swap():
        return remote(flipped, other, f_send, f_recv, me_p, me_q + 1 - 2 * core)

    def t_turn():
        @pl.loop(0, size // wide)
        def _(b):
            first = pl.multiple_of(b * wide, wide)
            part = pl.ds(first, wide)
            block = tile[part, :].T
            spot = lax.broadcasted_iota(jnp.int32, block.shape, 1) + first
            flipped[:, part] = jnp.where(spot < live, block, jnp.zeros_like(block))

        f_swap().start()

    def t_out(j):
        return remote(
            turned.at[j], tside.at[me_q], td_send.at[j], td_recv.at[me_q], t_to, j
        ), jnp.logical_and(t_to == me_p, j == me_q)

    def t_send(group):
        for spot in group:
            j = tile_at(*spot)
            copy, itself = t_out(j)

            @pl.when(itself)
            def _():
                pltpu.make_async_copy(turned.at[j], tside.at[me_q], td_recv.at[me_q]).start()

            @pl.when(jnp.logical_not(itself))
            def _():
                copy.start()

    def t_up(n, i):
        off, parent = t_nodes[n]
        return remote(
            tout.at[n - 1, :, t_cut[i]], tch.at[n - 1, :, t_cut[i]],
            tc_send.at[n - 1, i], tc_recv.at[n - 1, i],
            plane(t_nodes[parent][0] - off), me_q,
        )

    def t_sum(n, i):
        part = t_cut[i]
        total = None
        for off in t_sides[n]:
            if i == 0:
                arrived(tside.at[off % nt], td_recv.at[off % nt])
            piece = tside[off % nt, :, part].astype(F32)
            total = piece if total is None else total + piece
        for m, (_, parent) in enumerate(t_nodes):
            if parent == n:
                arrived(tch.at[m - 1, :, part], tc_recv.at[m - 1, i])
                total = total + tch[m - 1, :, part].astype(F32)
        return total

    def t_node(n):
        for i in range(T_PARTS):
            tout[n - 1, :, t_cut[i]] = t_sum(n, i).astype(BF16)
            t_up(n, i).start()

    blocks = size // wide
    d_cut = [(0, blocks - blocks // 2), (blocks - blocks // 2, blocks)][: min(blocks, 2)]

    def d_part(i):
        return pl.ds(d_cut[i][0] * wide, (d_cut[i][1] - d_cut[i][0]) * wide)

    def d_out(dy, db, i):
        m = chip_at(dy, db)
        return remote(
            dsend.at[m, :, d_part(i)], drecv.at[chip, :, d_part(i)],
            dd_send.at[m, i], dd_recv.at[chip, i], me_p, 2 * m + core,
        )

    def d_share(i):
        for dy, db in moves:
            d_out(dy, db, i).start()

    half = nt * share // 2

    def d_product(second):
        e = 1 - core if second else core
        for m in range(nt // 2):
            arrived(vsrc.at[e, m], vd_recv.at[e, m])
        if second:
            arrived(other, f_recv)
        source = vsrc[e].reshape(half, size)

        def columns(b):
            part = pl.ds(pl.multiple_of(b * wide, wide), wide)
            block = other[:, part] if second else flipped[:, part]
            prod = jnp.dot(source, block, preferred_element_type=F32).reshape(-1, share, wide)
            if second:
                prod = prod + dpart[:, :, part]
                dsend[:, :, part] = prod.astype(BF16)
            dpart[:, :, part] = prod

        if second:
            for i, (first, last) in enumerate(d_cut):
                pl.loop(first, last)(columns)
                d_share(i)
        else:
            pl.loop(0, size // wide)(columns)

    rank = jnp.int32(0)
    for n, offs in enumerate(t_sides):
        for off in offs:
            rank = rank + jnp.where(me_q == off % nt, min(abs(t_nodes[n][0]) // 3, 2), 0)
    at = [0, 0, 0]
    for word, number in PLAN if nt == 16 else SMALL:
        if word == "v":
            v_stage(number)
            v_deliver(number)
        elif word == "vf":
            v_stage(number)
        elif word == "vd":
            v_deliver(number)
        elif word == "greeted":
            pl.semaphore_wait(barrier, expected)
        elif word == "product":
            t_product()
        elif word == "turn":
            t_turn()
        elif word in ("near", "mid", "far"):
            k = ("near", "mid", "far").index(word)
            sent, at[k] = spots[at[k] : at[k] + number], at[k] + number

            @pl.when(rank == k)
            def _():
                t_send(sent)
        elif word == "node":
            t_node(number)
        elif word == "d":
            d_product(number)

    line = lax.broadcasted_iota(jnp.int32, (share, 128), 0)
    lane = lax.broadcasted_iota(jnp.int32, (share, 128), 1)

    def as_row(column, slot):
        return jnp.sum(jnp.where(lane == line + slot * share, column, 0.0), axis=0, keepdims=True)

    def as_column(row):
        return jnp.sum(jnp.where(lane == line, row, 0.0), axis=1, keepdims=True)

    load_energy.wait()
    load_bprev.wait()
    load_prev.wait()
    square = [lax.broadcasted_iota(jnp.int32, (share, share), d) for d in range(2)]
    before = jnp.where(square[0] == square[1], bprev_ref[...].reshape(1, share), 0.0)
    before = jnp.sum(before, axis=1, keepdims=True)
    own = vt[me_q].astype(F32)
    diagonal = energy_ref[...].reshape(1, size) * own
    behind = before * prev[...]
    norm = jnp.sum(own * own, axis=1, keepdims=True)
    back = jnp.sum(own * behind, axis=1, keepdims=True)

    total = jnp.concatenate([t_sum(0, i) for i in range(T_PARTS)], axis=1)
    total = total + dpart[chip]
    for dy, db in moves:
        m = chip_at(dy, db)
        for i in range(len(d_cut)):
            arrived(drecv.at[m, :, d_part(i)], dd_recv.at[m, i])
        total = total + drecv[m].astype(F32)

    hv = total + diagonal
    w = hv - behind
    numer = jnp.sum(own * hv, axis=1, keepdims=True)
    slope = (numer - back) / jnp.where(norm > 0.0, norm, 1.0)
    rest = w - slope * own
    rest = jnp.sum(rest * rest, axis=1, keepdims=True)
    row_out[0] = as_row(numer, 0) + as_row(norm, 1) + as_row(slope, 2) + as_row(rest, 3)
    for da, dz in others:
        remote(row_out.at[0], rows_in.at[me_p], s_send, s_recv, segment(da, dz), me_q).start()
    rows_in[me_p] = row_out[0]
    arrived(rows_in.at[pl.ds(0, nd - 1)], s_recv)

    rows = rows_in[...].reshape(nd, 128)
    norms = pltpu.roll(rows, 128 - share, 1)
    slopes = pltpu.roll(rows, 128 - 2 * share, 1)
    rests = pltpu.roll(rows, 128 - 3 * share, 1)
    alpha = jnp.sum(rows, axis=0, keepdims=True) / jnp.sum(norms, axis=0, keepdims=True)
    gap = slopes - alpha
    squared = jnp.sum(rests + gap * norms * gap, axis=0, keepdims=True)
    beta = jnp.sqrt(squared / rows_total + 1e-06)
    alpha_ref[...] = alpha
    beta_ref[...] = beta
    out_ref[...] = (w - as_column(alpha) * own) / as_column(beta)

    for n in range(len(v_nodes)):
        for off in v_sides[n]:
            copy, _, itself = v_out(n, off)

            @pl.when(jnp.logical_not(itself))
            def _():
                copy.wait_send()

        if n > 0:
            for i in range(V_PARTS):
                v_hop(n, i).wait_send()
    for n in range(1, len(t_nodes)):
        for i in range(T_PARTS):
            t_up(n, i).wait_send()
    for j in range(nt):
        copy, itself = t_out(j)

        @pl.when(jnp.logical_not(itself))
        def _():
            copy.wait_send()

    f_swap().wait_send()
    for dy, db in moves:
        for i in range(len(d_cut)):
            d_out(dy, db, i).wait_send()
    arrived(rows_in.at[pl.ds(0, nd - 1)], s_send)


def body(tiles, live_groups, vectors, previous, energies, beta_prev):
    nt = lax.axis_size("tile")
    nd = lax.axis_size("diag")
    size, columns = vectors.shape
    share = columns // nt
    v_tree, t_tree = trees_of(nt)
    v_more, t_more = max(len(v_tree[0]) - 1, 1), max(len(t_tree[0]) - 1, 1)
    vmem = pl.BlockSpec(memory_space=pltpu.VMEM)
    hbm = pl.BlockSpec(memory_space=pl.ANY)
    dma = pltpu.SemaphoreType.DMA
    out, alpha, beta = pl.pallas_call(
        functools.partial(kernel, nt, v_tree, t_tree, float(size * nd)),
        out_shape=(
            jax.ShapeDtypeStruct((share, size), F32),
            jax.ShapeDtypeStruct((1, 128), F32),
            jax.ShapeDtypeStruct((1, 128), F32),
        ),
        in_specs=[hbm] * 6,
        out_specs=(vmem, vmem, vmem),
        scratch_shapes=[
            pltpu.SMEM((1, 1), jnp.int32),
            pltpu.VMEM((size,), F32),
            pltpu.VMEM((share,), F32),
            pltpu.VMEM((size, columns), BF16),
            pltpu.VMEM((share, size), F32),
            pltpu.VMEM((size, size), BF16),
            pltpu.VMEM((size, size), BF16),
            pltpu.VMEM((size, size), BF16),
            pltpu.VMEM((nt, share, size), BF16),
            pltpu.VMEM((2, nt // 2, share, size), BF16),
            pltpu.VMEM((nt, share, size), BF16),
            pltpu.VMEM((nt, share, size), BF16),
            pltpu.VMEM((nt // 2, share, size), F32),
            pltpu.VMEM((nt // 2, share, size), BF16),
            pltpu.VMEM((nt // 2, share, size), BF16),
            pltpu.VMEM((v_more, share, size), BF16),
            pltpu.VMEM((t_more, share, size), BF16),
            pltpu.VMEM((t_more, share, size), BF16),
            pltpu.VMEM((1, 1, 128), F32),
            pltpu.VMEM((nd, 1, 128), F32),
            dma, dma, dma, dma, dma, dma,
            dma((nt,)), dma((2, nt // 2)), dma((v_more, V_PARTS)), dma((v_more, V_PARTS)),
            dma((nt,)), dma((nt,)), dma((t_more, T_PARTS)), dma((t_more, T_PARTS)),
            dma, dma, dma((nt // 2, 2)), dma((nt // 2, 2)),
            dma, dma,
        ],
        compiler_params=pltpu.CompilerParams(
            collective_id=0, has_side_effects=True, vmem_limit_bytes=VMEM_KIB * 1024
        ),
    )(live_groups, energies, beta_prev, vectors, previous.T, tiles)
    return out.T, alpha[0, :share], beta[0, :share]


def solution(mesh):
    return jax.shard_map(
        body,
        mesh=mesh,
        in_specs=(
            P("diag", "tile", None, None),
            P("diag", "tile"),
            P("diag", None),
            P("diag", "tile"),
            P("diag"),
            P("tile"),
        ),
        out_specs=(P("diag", "tile"), P("tile"), P("tile")),
        check_vma=False,
    )
```
